32 devices in a mesh: shard: 8 (over y, x, core), tensor: 4 (over z).
Axes of the slice: x: 2, y: 2, z: 4, core: 2. Of those that a mesh axis runs over, the one named last changes fastest.
Arguments:
- tokens: bfloat16 [3072, 1024], P(('shard', 'tensor')), may hold values from -6 to 6
- doc_starts: int32 [2], replicated, may hold values from 0 to 3071, as said below
- norm1_gain: float32 [1024], replicated, may hold values from 0.25 to 1.75
- qkv_weight: bfloat16 [1024, 3, 1024], P('shard', None, 'tensor'), may hold values from -0.25 to 0.25
- out_weight: bfloat16 [1024, 1024], P('shard', 'tensor'), may hold values from -1.25 to 1.25
- norm2_gain: float32 [1024], replicated, may hold values from 0.25 to 1.75
- in_weight: bfloat16 [1024, 2, 2624], P('shard', None, 'tensor'), may hold values from -0.1875 to 0.1875
- down_weight: bfloat16 [1024, 2624], P('shard', 'tensor'), may hold values from -0.25 to 0.25
- cotangent: bfloat16 [3072, 1024], P(('shard', 'tensor')), may hold values from -8 to 8
Outputs:
- mixed: bfloat16 [3072, 1024], P(('shard', 'tensor'))
- tokens_grad: bfloat16 [3072, 1024], P(('shard', 'tensor'))
- norm1_gain_grad: float32 [1024], replicated
- qkv_weight_grad: float32 [1024, 3, 1024], P('shard', None, 'tensor')
- out_weight_grad: float32 [1024, 1024], P('shard', 'tensor')
- norm2_gain_grad: float32 [1024], replicated
- in_weight_grad: float32 [1024, 2, 2624], P('shard', None, 'tensor')
- down_weight_grad: float32 [1024, 2624], P('shard', 'tensor')
The draws below stay inside these ranges and needn't reach their ends.
Inputs may be any that keep to these rules, and one draw needn't show every extreme that they name: doc_starts rises strictly from 0; the second document begins within the last 192 tokens; no document is longer than 3072 tokens.
All inputs are finite; a program needn't handle non-finite values.
Results may differ from the reference program's by a relative error of at most 0.04.
Values may be sent and summed in bfloat16 or wider, within the bound.
A program may use at most 192 MiB of HBM per device.

```python
import math
import jax
import jax.numpy as jnp
from jax import lax

D = 1024
HEADS = 16
HEAD_DIM = 64
FF = 2624
TOK_GROUP = 384
SEQ_LEN = 8192
TOKENS = 3072


def draw_doc_starts(key, part):
    key = jax.random.fold_in(key, 11)
    spacing = min(SEQ_LEN, TOKENS)
    nominal = TOKENS // spacing
    halfway = TOK_GROUP // 2
    leftover = jax.random.permutation(key, jnp.arange(1, halfway, dtype=jnp.int32))
    offsets = jnp.sort(leftover[:nominal])
    marks = jnp.arange(1, nominal + 1, dtype=jnp.int32) * spacing - offsets
    return jnp.concatenate([jnp.zeros((1,), jnp.int32), marks]).astype(jnp.int32)


def draw_cotangent(key, part):
    key = jax.random.fold_in(key, 23)
    stretch = jnp.arange(TOKENS, dtype=jnp.float32)[:, None] / TOKENS
    noise = jax.random.truncated_normal(key, -4.0, 4.0, (TOKENS, D), jnp.float32)
    return (noise * (0.6 + 1.4 * stretch)).astype(jnp.bfloat16)


def steps_of(rng, dims, cuts, smallest, high):
    factor_of = 1.0
    for dim, parts in cuts:
        steps = jax.random.uniform(jax.random.fold_in(jax.random.fold_in(rng, 6), dim), (parts,), jnp.float32, smallest / len(cuts), high / len(cuts))
        factor_of = factor_of * jnp.repeat(jnp.exp(steps), dims[dim] // parts).reshape((-1,) + (1,) * (len(dims) - 1 - dim))
    return factor_of


def scatter_about(key, shape, deviation, limit, shards=(), kind=jnp.bfloat16):
    loudness = steps_of(key, shape, shards, -0.22, 0.18) if shards else 1.0
    values = jax.random.normal(key, shape, jnp.float32) * deviation * loudness
    return jnp.minimum(jnp.maximum(values, -limit), limit).astype(kind)


def setup_inputs(seed: int = 0) -> dict:
    key_list = jax.random.split(jax.random.key(seed), 10)
    return {
        "tokens": scatter_about(key_list[0], (TOKENS, D), 1.0, 6.0, ((0, 32),)),
        "doc_starts": draw_doc_starts(jax.random.fold_in(key_list[9], 71), 0),
        "norm1_gain": jnp.clip(1.0 + 0.15 * jax.random.normal(key_list[2], (D,), jnp.float32), 0.25, 1.75),
        "qkv_weight": scatter_about(key_list[3], (D, 3, D), (D // 2) ** -0.5, 0.25, ((0, 8), (2, 4))),
        "out_weight": scatter_about(key_list[4], (D, D), (max(1, 64 * D // TOKENS)) ** -0.5, 1.25, ((0, 8), (1, 4))),
        "norm2_gain": jnp.clip(1.0 + 0.15 * jax.random.normal(key_list[5], (D,), jnp.float32), 0.25, 1.75),
        "in_weight": scatter_about(key_list[6], (D, 2, FF), D ** -0.5, 0.1875, ((0, 8), (2, 4))),
        "down_weight": scatter_about(key_list[7], (D, FF), (FF // 4) ** -0.5, 0.25, ((0, 8), (1, 4))),
        "cotangent": draw_cotangent(jax.random.fold_in(key_list[9], 71), 0),
    }


EPSILON = 1e-05
THETA = 160000.0
MASKED = -1e+30

@jax.custom_vjp
def low(v):
    return lax.optimization_barrier(v.astype(jnp.bfloat16)).astype(jnp.float32)

@jax.custom_vjp
def low_back(v):
    return v

def low_keep(v):
    return (low(v), None)

def low_pass(kept, grad):
    return (grad,)

def back_keep(v):
    return (v, None)

def back_low(kept, grad):
    return (low(grad),)
low.defvjp(low_keep, low_pass)
low_back.defvjp(back_keep, back_low)

def norm_rows(values, gain):
    centred = values - lax.optimization_barrier(jnp.mean(values, axis=-1, keepdims=True))
    variance = lax.optimization_barrier(jnp.mean(centred * centred, axis=-1, keepdims=True))
    return centred * lax.rsqrt(variance + EPSILON) * gain

def doc_layout(index, doc_starts):
    begun = doc_starts[None, :] <= index[:, None]
    segment = lax.optimization_barrier(jnp.sum(begun.astype(jnp.int32), axis=1)) - 1
    opening = lax.optimization_barrier(jnp.max(jnp.where(begun, doc_starts[None, :], 0), axis=1))
    return (segment, index - opening)

def turning(position, head_width):
    halfway = head_width // 2
    inverse = THETA ** (-jnp.arange(halfway, dtype=jnp.float32) * 2.0 / head_width)
    angles = position.astype(jnp.float32)[:, None] * inverse[None, :]
    return (jnp.cos(angles)[:, None, :], jnp.sin(angles)[:, None, :])

def rotate(values, cosine, sine, direction):
    halfway = values.shape[-1] // 2
    leading = values[..., :halfway]
    trailing = values[..., halfway:]
    return jnp.concatenate([leading * cosine - direction * trailing * sine, trailing * cosine + direction * leading * sine], axis=-1)

def query_block(query_rows, segment_rows, keys, values, segment):
    scores = jnp.einsum('qhe,khe->hqk', query_rows, keys, precision=lax.Precision.HIGHEST) * HEAD_DIM ** (-0.5)
    scores = low_back(scores)
    shared = segment_rows[:, None] == segment[None, :]
    scores = jnp.where(shared[None], scores, MASKED)
    highest = lax.optimization_barrier(jnp.max(scores, axis=-1, keepdims=True))
    weights = jnp.exp(scores - highest)
    weights = low(weights / lax.optimization_barrier(jnp.sum(weights, axis=-1, keepdims=True)))
    return jnp.einsum('hqk,khe->qhe', weights, values, precision=lax.Precision.HIGHEST)

def attention(query, keys, values, segment):
    token_count = query.shape[0]
    block_rows = math.gcd(token_count, 512)
    blocked = (query.reshape(token_count // block_rows, block_rows, HEADS, HEAD_DIM), segment.reshape(token_count // block_rows, block_rows))
    checked = jax.checkpoint(query_block)

    def advance(running, entries):
        return (running, checked(entries[0], entries[1], keys, values, segment))
    _, outputs = lax.scan(advance, jnp.zeros((), jnp.float32), blocked)
    return outputs.reshape(token_count, HEADS, HEAD_DIM)

def reference(tokens, doc_starts, norm1_gain, qkv_weight, out_weight, norm2_gain, in_weight, down_weight, cotangent):
    index = jnp.arange(tokens.shape[0], dtype=jnp.int32)
    segment, position = doc_layout(index, doc_starts)
    cosine, sine = turning(position, HEAD_DIM)

    def forward(resid_in, gain_one, qkv_mat, out_mat, gain_two, in_mat, down_mat):
        token_count = resid_in.shape[0]
        normed_one = low(norm_rows(resid_in, gain_one))
        projected = jnp.einsum('td,dke->tke', normed_one, qkv_mat, precision=lax.Precision.HIGHEST)
        query_raw = low_back(projected[:, 0]).reshape(token_count, HEADS, HEAD_DIM)
        key_raw = low_back(projected[:, 1]).reshape(token_count, HEADS, HEAD_DIM)
        values = low(low_back(projected[:, 2])).reshape(token_count, HEADS, HEAD_DIM)
        query = low(rotate(query_raw, cosine, sine, 1.0))
        keys = low(rotate(key_raw, cosine, sine, 1.0))
        attended = attention(query, keys, values, segment).reshape(token_count, D)
        attended = low(low_back(attended))
        resid_mid = resid_in + low_back(jnp.dot(attended, out_mat.T, precision=lax.Precision.HIGHEST))
        normed_two = low(norm_rows(resid_mid, gain_two))
        gate_up = jnp.einsum('td,dke->tke', normed_two, in_mat, precision=lax.Precision.HIGHEST)
        gate = low_back(gate_up[:, 0])
        upward = low_back(gate_up[:, 1])
        active = low(jax.nn.gelu(gate, approximate=False) * upward)
        return resid_mid + jnp.dot(active, down_mat.T, precision=lax.Precision.HIGHEST)
    primals = (tokens.astype(jnp.float32), norm1_gain.astype(jnp.float32), qkv_weight.astype(jnp.float32), out_weight.astype(jnp.float32), norm2_gain.astype(jnp.float32), in_weight.astype(jnp.float32), down_weight.astype(jnp.float32))
    mixed, pullback = jax.vjp(forward, *primals)
    gradients = pullback(cotangent.astype(jnp.float32))
    return (mixed.astype(jnp.bfloat16), gradients[0].astype(jnp.bfloat16), gradients[1], gradients[2], gradients[3], gradients[4], gradients[5], gradients[6])
```

```python
import jax
import jax.numpy as jnp
from jax import lax
from jax.experimental import pallas as pl
from jax.experimental.pallas import tpu as pltpu
from jax.sharding import PartitionSpec as P

HEAD_DIM = 64
EPSILON = 1e-05
THETA = 160000.0
MASKED = -1e30
MESH = pl.DeviceIdType.MESH
VMEM_BYTES = 56 * 1024 * 1024
FWD_CHUNK = 512
BWD_CHUNK = 256


def norm_rows(values, gain):
    centred = values - jnp.mean(values, axis=-1, keepdims=True)
    variance = jnp.mean(centred * centred, axis=-1, keepdims=True)
    return centred * lax.rsqrt(variance + EPSILON) * gain


def doc_layout(index, doc_starts):
    begun = doc_starts[None, :] <= index[:, None]
    segment = jnp.sum(begun.astype(jnp.int32), axis=1) - 1
    opening = jnp.max(jnp.where(begun, doc_starts[None, :], 0), axis=1)
    return (segment, index - opening)


def turning(position, head_width):
    halfway = head_width // 2
    inverse = THETA ** (-jnp.arange(halfway, dtype=jnp.float32) * 2.0 / head_width)
    angles = position.astype(jnp.float32)[:, None] * inverse[None, :]
    return (jnp.cos(angles)[:, None, :], jnp.sin(angles)[:, None, :])


def rotate(values, cosine, sine, direction):
    halfway = values.shape[-1] // 2
    leading = values[..., :halfway]
    trailing = values[..., halfway:]
    return jnp.concatenate(
        [
            leading * cosine - direction * trailing * sine,
            trailing * cosine + direction * leading * sine,
        ],
        axis=-1,
    )


def geglu(gate, upward):
    return jax.nn.gelu(gate, approximate=False) * upward


class Transfers:
    def __init__(self, items):
        self.items = items
        self.sizes = [lax.axis_size(axis) for _, axis, _ in items]

    def shapes(self):
        shapes = []
        for (value, _, kind), size in zip(self.items, self.sizes):
            if kind in ("gather", "spread"):
                shape = (size,) + value.shape
            else:
                shape = value.shape
            shapes.append(jax.ShapeDtypeStruct(shape, value.dtype))
        return shapes

    def scratch(self):
        semaphores = []
        for size in self.sizes:
            semaphores += [pltpu.SemaphoreType.DMA((2 * size,)), pltpu.SemaphoreType.DMA((2 * size,))]
        return semaphores + [pltpu.SemaphoreType.DMA((len(self.items),))]

    def barrier(self):
        barrier = pltpu.get_barrier_semaphore()
        total = 0
        for axis in ("shard", "tensor"):
            if any(other == axis for _, other, _ in self.items):
                size = lax.axis_size(axis)
                me = lax.axis_index(axis)
                for step in range(1, size):
                    pl.semaphore_signal(
                        barrier,
                        inc=1,
                        device_id={axis: lax.rem(me + step, size)},
                        device_id_type=MESH,
                    )
                total += size - 1
        pl.semaphore_wait(barrier, total)

    def start(self, in_refs, out_refs, sems):
        self.barrier()
        local_sem = sems[-1]
        self.sent, self.landing, self.passing = [], [], []
        for place, (_, axis, kind) in enumerate(self.items):
            source, target = in_refs[place], out_refs[place]
            send, recv = sems[2 * place], sems[2 * place + 1]
            size = self.sizes[place]
            me = lax.axis_index(axis)

            def post(src, dst, slot, peer, axis=axis, send=send, recv=recv):
                copy = pltpu.make_async_remote_copy(
                    src_ref=src,
                    dst_ref=dst,
                    send_sem=send.at[slot],
                    recv_sem=recv.at[slot],
                    device_id={axis: peer},
                    device_id_type=MESH,
                )
                return copy

            if kind == "gather" or kind == "swap":
                for step in range(1, size):
                    peer, origin = lax.rem(me + step, size), lax.rem(me + size - step, size)
                    src = source if kind == "gather" else source.at[peer]
                    copy = post(src, target.at[me], step, peer)
                    copy.start()
                    self.sent.append(copy)
                    self.landing.append(post(src, target.at[origin], step, peer))
                own = source if kind == "gather" else source.at[me]
                keep = pltpu.make_async_copy(own, target.at[me], local_sem.at[place])
                keep.start()
                self.sent.append(keep)
            else:
                chips = size // 2
                chip, core = lax.div(me, 2), lax.rem(me, 2)
                partner = me + 1 - 2 * core
                if kind == "pair":
                    copy = post(source.at[1 - core], target.at[1 - core], 0, partner)
                    copy.start()
                    self.sent.append(copy)
                    self.landing.append(post(source.at[core], target.at[core], 0, partner))
                    keep = pltpu.make_async_copy(
                        source.at[core], target.at[1 - core], local_sem.at[place]
                    )
                    keep.start()
                    self.sent.append(keep)
                    continue
                for step in range(1, chips):
                    far, origin = lax.rem(chip + step, chips), lax.rem(chip + chips - step, chips)
                    peer = 2 * far + core
                    if kind == "spread":
                        copy = post(source, target.at[me], step, peer)
                        block = target.at[2 * origin + core]
                        other = target.at[2 * origin + 1 - core]
                        arrive = post(source, block, step, peer)
                        onward = post(block, block, size + step, partner)
                        self.passing.append(
                            (arrive, onward, post(block, other, size + step, partner))
                        )
                    else:
                        copy = post(source.at[far], target.at[chip], step, peer)
                        self.landing.append(
                            post(source.at[far], target.at[origin], step, peer)
                        )
                    copy.start()
                    self.sent.append(copy)
                if kind == "spread":
                    copy = post(source, target.at[me], 0, partner)
                    copy.start()
                    self.sent.append(copy)
                    self.landing.append(post(source, target.at[partner], 0, partner))
                    keep = pltpu.make_async_copy(source, target.at[me], local_sem.at[place])
                else:
                    keep = pltpu.make_async_copy(
                        source.at[chip], target.at[chip], local_sem.at[place]
                    )
                keep.start()
                self.sent.append(keep)

    def finish(self):
        for arrive, onward, _ in self.passing:
            arrive.wait_recv()
            onward.start()
        for _, onward, other in self.passing:
            onward.wait_send()
            other.wait_recv()
        for copy in self.landing:
            copy.wait_recv()
        for copy in self.sent:
            if hasattr(copy, "wait_send") and copy.is_remote:
                copy.wait_send()
            else:
                copy.wait()


ANY = pl.BlockSpec(memory_space=pl.ANY)
WHOLE = pl.BlockSpec(memory_space=pltpu.VMEM)


def run_kernel(ident, name, moves, work=None, arrays=(), results=(), scratch=(), cost=None):
    transfers = Transfers(moves)
    carried, count = len(moves), len(arrays)

    def kernel(*refs):
        refs = list(refs)
        array_refs, in_refs = refs[:count], refs[count : count + carried]
        refs = refs[count + carried :]
        result_refs, out_refs = refs[: len(results)], refs[len(results) : len(results) + carried]
        refs = refs[len(results) + carried :]
        scratch_refs, sems = refs[: len(scratch)], refs[len(scratch) :]
        transfers.start(in_refs, out_refs, sems)
        if work is not None:
            work(*array_refs, *result_refs, *scratch_refs)
        transfers.finish()

    return pl.pallas_call(
        kernel,
        out_shape=tuple(results) + tuple(transfers.shapes()),
        in_specs=[WHOLE] * count + [ANY] * carried,
        out_specs=tuple([WHOLE] * len(results) + [ANY] * carried),
        scratch_shapes=list(scratch) + transfers.scratch(),
        compiler_params=pltpu.CompilerParams(
            collective_id=ident,
            has_side_effects=True,
            vmem_limit_bytes=VMEM_BYTES if work is not None else None,
        ),
        cost_estimate=cost,
        name=name,
    )(*arrays, *[value for value, _, _ in moves])


def attend_forward(
    keys_values, turned_pairs, turned_query, key_segment, query_segment, out, log_total, held
):
    total = keys_values.shape[0]
    wide = turned_query.shape[1]
    held[...] = jnp.zeros_like(held)
    query = turned_query[...]
    mine = query_segment[...]

    def step(index, carry):
        highest, summed = carry
        rows = pl.ds(pl.multiple_of(index * FWD_CHUNK, FWD_CHUNK), FWD_CHUNK)
        scores = jnp.dot(keys_values[rows, :], query, preferred_element_type=jnp.float32)
        scores = jnp.where(key_segment[rows, :] == mine, scores, MASKED)
        raised = jnp.maximum(highest, jnp.max(scores, axis=0, keepdims=True))
        lowered = jnp.exp(highest - raised)
        weights = jnp.exp(scores - raised)
        summed = summed * lowered + jnp.sum(weights, axis=0, keepdims=True)
        held[...] = held[...] * lowered + jnp.dot(
            turned_pairs[HEAD_DIM:, rows],
            weights.astype(jnp.bfloat16),
            preferred_element_type=jnp.float32,
        )
        return (raised, summed)

    highest, summed = lax.fori_loop(
        0,
        total // FWD_CHUNK,
        step,
        (jnp.full((1, wide), MASKED, jnp.float32), jnp.zeros((1, wide), jnp.float32)),
    )
    out[...] = held[...] / summed
    log_total[...] = highest + jnp.log(summed)


def attend_backward(
    keys_values,
    turned_pairs,
    turned_query,
    turned_grad,
    query_wide,
    grad_wide,
    key_segment,
    query_segment,
    log_total,
    attended,
    pair_grad,
    query_grad,
):
    total = keys_values.shape[0]
    query_grad[...] = jnp.zeros_like(query_grad)
    query = turned_query[...]
    grad = turned_grad[...]
    mine = query_segment[...]
    logs = log_total[...]
    delta = jnp.sum(grad[HEAD_DIM:, :].astype(jnp.float32) * attended[...], axis=0, keepdims=True)

    def step(index, carry):
        rows = pl.ds(pl.multiple_of(index * BWD_CHUNK, BWD_CHUNK), BWD_CHUNK)
        pairs = keys_values[rows, :]
        scores = jnp.dot(pairs, query, preferred_element_type=jnp.float32)
        weights = jnp.exp(
            jnp.where(key_segment[rows, :] == mine, scores - logs, MASKED)
        )
        weight_grad = jnp.dot(pairs, grad, preferred_element_type=jnp.float32)
        score_grad = (weights * (weight_grad - delta)).astype(jnp.bfloat16)
        pair_grad[rows, :] = (
            jnp.dot(score_grad, query_wide[...], preferred_element_type=jnp.float32)
            + jnp.dot(
                weights.astype(jnp.bfloat16), grad_wide[...], preferred_element_type=jnp.float32
            )
        ).astype(pair_grad.dtype)
        query_grad[...] += jnp.dot(
            turned_pairs[:HEAD_DIM, rows], score_grad, preferred_element_type=jnp.float32
        )
        return carry

    lax.fori_loop(0, total // BWD_CHUNK, step, 0)


def fold_rows(values, padded):
    half = values.shape[-2] // 2
    folded = jnp.concatenate([values[..., :half, :], values[..., half:, :]], axis=-1)
    extra = padded - half
    if extra:
        folded = jnp.pad(folded, [(0, 0)] * (folded.ndim - 2) + [(0, extra), (0, 0)])
    return folded


def unfold_rows(folded, half):
    folded = folded[..., :half, :]
    return jnp.concatenate([folded[..., :HEAD_DIM], folded[..., HEAD_DIM:]], axis=-2)


def on_device(
    tokens,
    doc_starts,
    norm1_gain,
    qkv_weight,
    out_weight,
    norm2_gain,
    in_weight,
    down_weight,
    cotangent,
):
    row_count, model_width = tokens.shape
    local_width = qkv_weight.shape[2]
    unit_width = in_weight.shape[2]
    head_dim = HEAD_DIM
    heads = local_width // head_dim
    shards = lax.axis_size("shard")
    tensors = lax.axis_size("tensor")
    me_shard = lax.axis_index("shard")
    group_rows = row_count * tensors
    all_rows = group_rows * shards
    parts = shards // heads
    part_rows = group_rows // parts
    half = part_rows // 2
    padded = -(-half // 16) * 16
    query_rows = shards * part_rows
    group_index = me_shard * group_rows + jnp.arange(group_rows, dtype=jnp.int32)
    segment, position = doc_layout(group_index, doc_starts)
    cosine, sine = turning(position, head_dim)
    contract_rows = (((0,), (0,)), ((), ()))
    contract_cols = (((1,), (1,)), ((), ()))
    shape_heads = (group_rows, heads, head_dim)
    bf16, f32 = jnp.bfloat16, jnp.float32

    def to_parts(values):
        return (
            values.reshape(parts, part_rows, heads, head_dim)
            .transpose(2, 0, 1, 3)
            .reshape(shards, part_rows, head_dim)
        )

    def from_parts(values):
        return (
            values.reshape(heads, parts, part_rows, head_dim)
            .transpose(1, 2, 0, 3)
            .reshape(group_rows, local_width)
        )

    resid_in = tokens.astype(f32)
    normed_one, norm_one_back = jax.vjp(norm_rows, resid_in, norm1_gain)
    rows_one, qkv_full = run_kernel(
        1,
        "gather_inputs",
        [
            (normed_one.astype(bf16), "tensor", "gather"),
            (qkv_weight.reshape(-1, 3 * local_width), "shard", "spread"),
        ],
    )
    rows_one = rows_one.reshape(group_rows, model_width)
    qkv_mat = qkv_full.reshape(model_width, 3 * local_width)
    projected = jnp.dot(rows_one, qkv_mat, preferred_element_type=f32)
    score_scale = head_dim ** (-0.5)
    query = rotate(projected[:, :local_width].reshape(shape_heads), cosine, sine, 1.0).astype(bf16)
    keys = rotate(
        projected[:, local_width : 2 * local_width].reshape(shape_heads), cosine, sine, 1.0
    ).astype(bf16)
    values = projected[:, 2 * local_width :].astype(bf16).reshape(shape_heads)
    pairs = jnp.concatenate([keys, values], axis=-1).transpose(1, 0, 2)
    pairs = jnp.broadcast_to(pairs[:, None], (heads, parts, group_rows, 2 * head_dim)).reshape(
        shards, group_rows, 2 * head_dim
    )
    folded_query = fold_rows(to_parts(query * jnp.asarray(score_scale, bf16)), padded)
    sent_qkv, out_full = run_kernel(
        2,
        "swap_heads",
        [
            (jnp.concatenate([pairs, folded_query], axis=1), "shard", "swap"),
            (out_weight, "shard", "spread"),
        ],
    )
    out_full = out_full.reshape(model_width, local_width)
    keys_values = sent_qkv[:, :group_rows].reshape(all_rows, 2 * head_dim)
    turned_pairs = keys_values.T
    query_mine = unfold_rows(sent_qkv[:, group_rows:], half).reshape(query_rows, head_dim)
    no_query = jnp.zeros_like(query_mine)
    query_wide = jnp.concatenate([query_mine, no_query], axis=1)
    turned_query = query_wide.T
    key_segment, _ = doc_layout(jnp.arange(all_rows, dtype=jnp.int32), doc_starts)
    mine = lax.rem(me_shard, parts) * part_rows
    query_segment = lax.dynamic_slice_in_dim(
        key_segment.reshape(shards, group_rows), mine, part_rows, axis=1
    ).reshape(1, query_rows)
    key_segment = key_segment.reshape(all_rows, 1)
    attended_turned, log_total, in_full, cot_full = run_kernel(
        3,
        "attend_forward",
        [
            (in_weight.reshape(-1, 2 * unit_width), "shard", "spread"),
            (cotangent, "tensor", "gather"),
        ],
        attend_forward,
        (keys_values, turned_pairs, turned_query, key_segment, query_segment),
        (
            jax.ShapeDtypeStruct((head_dim, query_rows), f32),
            jax.ShapeDtypeStruct((1, query_rows), f32),
        ),
        (pltpu.VMEM((head_dim, query_rows), f32),),
    )
    in_mat = in_full.reshape(model_width, 2 * unit_width)
    cot_full = cot_full.reshape(group_rows, model_width)
    attended_back = fold_rows(
        attended_turned.astype(bf16).T.reshape(shards, part_rows, head_dim), padded
    )
    (attended_parts,) = run_kernel(4, "return_heads", [(attended_back, "shard", "swap")])
    attended = from_parts(unfold_rows(attended_parts, half))

    def share(left, right):
        return (
            lax.dot_general(left, right, contract_cols, preferred_element_type=f32)
            .astype(bf16)
            .reshape(tensors, row_count, model_width)
        )

    out_parts, down_full = run_kernel(
        5,
        "out_shares",
        [(share(attended, out_full), "tensor", "swap"), (down_weight, "shard", "spread")],
    )
    down_full = down_full.reshape(model_width, unit_width)
    resid_mid = resid_in + jnp.sum(out_parts.astype(f32), axis=0)
    normed_two, norm_two_back = jax.vjp(norm_rows, resid_mid, norm2_gain)
    (rows_two,) = run_kernel(6, "gather_middle", [(normed_two.astype(bf16), "tensor", "gather")])
    rows_two = rows_two.reshape(group_rows, model_width)
    gate_up = jnp.dot(rows_two, in_mat, preferred_element_type=f32)
    active, geglu_back = jax.vjp(geglu, gate_up[:, :unit_width], gate_up[:, unit_width:])
    active = active.astype(bf16)
    active_grad = jnp.dot(cot_full, down_full, preferred_element_type=f32)
    gate_grad, up_grad = geglu_back(active_grad)
    gate_up_grad = jnp.concatenate([gate_grad, up_grad], axis=1).astype(bf16)
    in_grad = lax.dot_general(rows_two, gate_up_grad, contract_rows, preferred_element_type=f32)
    down_grad = lax.dot_general(cot_full, active, contract_rows, preferred_element_type=f32)

    def by_core(grad):
        return (
            grad.astype(bf16)
            .reshape(shards // 2, 2, model_width // shards, grad.shape[1])
            .transpose(1, 0, 2, 3)
        )

    two_parts, in_pair, down_pair = run_kernel(
        7,
        "middle_grad_shares",
        [
            (share(gate_up_grad, in_mat), "tensor", "swap"),
            (by_core(in_grad), "shard", "pair"),
            (by_core(down_grad), "shard", "pair"),
        ],
    )
    normed_two_grad = jnp.sum(two_parts.astype(f32), axis=0)
    mid_part, gain_two_grad = norm_two_back(normed_two_grad)
    mid_grad = cotangent.astype(f32) + mid_part
    (branch_full,) = run_kernel(
        8, "gather_branch", [(mid_grad.astype(bf16), "tensor", "gather")]
    )
    branch_full = branch_full.reshape(group_rows, model_width)
    out_grad = lax.dot_general(branch_full, attended, contract_rows, preferred_element_type=f32)
    attended_grad = jnp.dot(branch_full, out_full, preferred_element_type=f32).astype(bf16)
    (grad_parts,) = run_kernel(
        9,
        "swap_grads",
        [(fold_rows(to_parts(attended_grad.reshape(shape_heads)), padded), "shard", "swap")],
    )
    grad_mine = unfold_rows(grad_parts, half).reshape(query_rows, head_dim)
    grad_wide = jnp.concatenate([jnp.zeros_like(grad_mine), grad_mine], axis=1)

    def add_pair(pair):
        return jnp.sum(pair.astype(f32), axis=0).astype(bf16)

    by_shard = (shards, model_width // shards)
    pair_grad, query_grad_turned, mixed_parts, in_parts, down_parts, out_grads = run_kernel(
        10,
        "attend_backward",
        [
            (share(active, down_full), "tensor", "swap"),
            (add_pair(in_pair), "shard", "mates"),
            (add_pair(down_pair), "shard", "mates"),
            (out_grad.astype(bf16).reshape(*by_shard, local_width), "shard", "swap"),
        ],
        attend_backward,
        (
            keys_values,
            turned_pairs,
            turned_query,
            grad_wide.T,
            query_wide,
            grad_wide,
            key_segment,
            query_segment,
            log_total,
            attended_turned,
        ),
        (
            jax.ShapeDtypeStruct((all_rows, 2 * head_dim), bf16),
            jax.ShapeDtypeStruct((head_dim, query_rows), f32),
        ),
    )
    mixed = (resid_mid + jnp.sum(mixed_parts.astype(f32), axis=0)).astype(bf16)
    folded_grad = fold_rows(
        query_grad_turned.astype(bf16).T.reshape(shards, part_rows, head_dim), padded
    )
    (qkv_back,) = run_kernel(
        11,
        "return_grads",
        [
            (
                jnp.concatenate(
                    [pair_grad.reshape(shards, group_rows, 2 * head_dim), folded_grad], axis=1
                ),
                "shard",
                "swap",
            )
        ],
    )
    query_rot_grad = from_parts(unfold_rows(qkv_back[:, group_rows:], half)).reshape(shape_heads)
    pair_sum = jnp.sum(
        qkv_back[:, :group_rows].reshape(heads, parts, group_rows, 2 * head_dim).astype(f32), axis=1
    ).transpose(1, 0, 2)
    query_grad = rotate(query_rot_grad.astype(f32) * score_scale, cosine, sine, -1.0).astype(bf16)
    key_grad = rotate(pair_sum[..., :head_dim], cosine, sine, -1.0).astype(bf16)
    qkv_grad = jnp.concatenate(
        [
            query_grad.reshape(group_rows, local_width),
            key_grad.reshape(group_rows, local_width),
            pair_sum[..., head_dim:].astype(bf16).reshape(group_rows, local_width),
        ],
        axis=1,
    )
    qkv_grad_w = lax.dot_general(rows_one, qkv_grad, contract_rows, preferred_element_type=f32)
    one_share = lax.dot_general(qkv_grad, qkv_mat, contract_cols, preferred_element_type=f32)
    gain_one_share = jnp.sum(one_share * rows_one.astype(f32), axis=0) / norm1_gain
    gains = jnp.concatenate([gain_one_share, gain_two_grad]).reshape(-1, 128)
    one_parts, qkv_parts, gain_parts = run_kernel(
        12,
        "input_grad_shares",
        [
            (one_share.astype(bf16).reshape(tensors, row_count, model_width), "tensor", "swap"),
            (qkv_grad_w.astype(bf16).reshape(*by_shard, 3 * local_width), "shard", "swap"),
            (gains, "shard", "gather"),
        ],
    )
    (gain_all,) = run_kernel(
        13, "gather_gains", [(jnp.sum(gain_parts, axis=0), "tensor", "gather")]
    )
    gain_all = jnp.sum(gain_all, axis=0).reshape(2, model_width)
    normed_one_grad = jnp.sum(one_parts.astype(f32), axis=0)
    input_part, _ = norm_one_back(normed_one_grad)
    tokens_grad = (mid_grad + input_part).astype(bf16)

    def add_up(pieces, shape):
        return jnp.sum(pieces.astype(f32), axis=0).reshape(shape)

    return (
        mixed,
        tokens_grad,
        gain_all[0],
        add_up(qkv_parts, qkv_weight.shape),
        add_up(out_grads, out_weight.shape),
        gain_all[1],
        add_up(in_parts, in_weight.shape),
        add_up(down_parts, down_weight.shape),
    )


def solution(mesh):
    in_specs = (
        P(("shard", "tensor"), None),
        P(),
        P(),
        P("shard", None, "tensor"),
        P("shard", "tensor"),
        P(),
        P("shard", None, "tensor"),
        P("shard", "tensor"),
        P(("shard", "tensor"), None),
    )
    out_specs = (
        P(("shard", "tensor"), None),
        P(("shard", "tensor"), None),
        P(),
        P("shard", None, "tensor"),
        P("shard", "tensor"),
        P(),
        P("shard", None, "tensor"),
        P("shard", "tensor"),
    )
    return jax.shard_map(
        on_device, mesh=mesh, in_specs=in_specs, out_specs=out_specs, check_vma=False
    )
```

```python
import jax
import jax.numpy as jnp
from jax import lax
from jax.experimental import pallas as pl
from jax.experimental.pallas import tpu as pltpu
from jax.sharding import PartitionSpec as P

HEAD_DIM = 64
EPSILON = 1e-05
THETA = 160000.0
MASKED = -1e30
MESH = pl.DeviceIdType.MESH
VMEM_BYTES = 56 * 1024 * 1024
FWD_CHUNK = 1024
BWD_CHUNK = 512


def norm_rows(values, gain):
    centred = values - jnp.mean(values, axis=-1, keepdims=True)
    variance = jnp.mean(centred * centred, axis=-1, keepdims=True)
    return centred * lax.rsqrt(variance + EPSILON) * gain


def doc_layout(index, doc_starts):
    begun = doc_starts[None, :] <= index[:, None]
    segment = jnp.sum(begun.astype(jnp.int32), axis=1) - 1
    opening = jnp.max(jnp.where(begun, doc_starts[None, :], 0), axis=1)
    return (segment, index - opening)


def turning(position, head_width):
    halfway = head_width // 2
    inverse = THETA ** (-jnp.arange(halfway, dtype=jnp.float32) * 2.0 / head_width)
    angles = position.astype(jnp.float32)[:, None] * inverse[None, :]
    return (jnp.cos(angles)[:, None, :], jnp.sin(angles)[:, None, :])


def rotate(values, cosine, sine, direction):
    halfway = values.shape[-1] // 2
    leading = values[..., :halfway]
    trailing = values[..., halfway:]
    return jnp.concatenate(
        [
            leading * cosine - direction * trailing * sine,
            trailing * cosine + direction * leading * sine,
        ],
        axis=-1,
    )


def geglu(gate, upward):
    return jax.nn.gelu(gate, approximate=False) * upward


class Transfers:
    def __init__(self, items):
        self.items = items
        self.sizes = [lax.axis_size(axis) for _, axis, _ in items]

    def shapes(self):
        shapes = []
        for (value, _, kind), size in zip(self.items, self.sizes):
            if kind in ("gather", "spread"):
                shape = (size,) + value.shape
            else:
                shape = value.shape
            shapes.append(jax.ShapeDtypeStruct(shape, value.dtype))
        return shapes

    def scratch(self):
        semaphores = []
        for size in self.sizes:
            semaphores += [pltpu.SemaphoreType.DMA((4 * size,)), pltpu.SemaphoreType.DMA((4 * size,))]
        return semaphores + [pltpu.SemaphoreType.DMA((2 * len(self.items),))]

    def staging(self):
        blocks = []
        for value, _, kind in self.items:
            shape = value.shape if kind in ("gather", "spread") else value.shape[1:]
            if kind == "pair":
                shape = (16, 128)
            blocks.append(pltpu.VMEM(shape, value.dtype))
        return blocks

    def barrier(self):
        barrier = pltpu.get_barrier_semaphore()
        total = 0
        for axis in ("shard", "tensor"):
            if any(other == axis for _, other, _ in self.items):
                size = lax.axis_size(axis)
                me = lax.axis_index(axis)
                for step in range(1, size):
                    pl.semaphore_signal(
                        barrier,
                        inc=1,
                        device_id={axis: lax.rem(me + step, size)},
                        device_id_type=MESH,
                    )
                total += size - 1
        pl.semaphore_wait(barrier, total)

    def start(self, in_refs, out_refs, stages, sems, lead):
        local_sem = sems[-1]
        self.sent, self.landing, self.passing, self.kept = [], [], [], []

        def keep(place, source, target):
            inward = pltpu.make_async_copy(source, stages[place], local_sem.at[2 * place])
            inward.start()
            self.kept.append(
                (
                    inward,
                    pltpu.make_async_copy(stages[place], target, local_sem.at[2 * place + 1]),
                )
            )

        self.barrier()
        lead()
        for place, (_, axis, kind) in enumerate(self.items):
            source, target = in_refs[place], out_refs[place]
            send, recv = sems[2 * place], sems[2 * place + 1]
            size = self.sizes[place]
            me = lax.axis_index(axis)

            def post(src, dst, slot, peer, axis=axis, send=send, recv=recv):
                copy = pltpu.make_async_remote_copy(
                    src_ref=src,
                    dst_ref=dst,
                    send_sem=send.at[slot],
                    recv_sem=recv.at[slot],
                    device_id={axis: peer},
                    device_id_type=MESH,
                )
                return copy

            if kind == "gather" or kind == "swap":
                for step in range(1, size):
                    peer, origin = lax.rem(me + step, size), lax.rem(me + size - step, size)
                    src = source if kind == "gather" else source.at[peer]
                    copy = post(src, target.at[me], step, peer)
                    copy.start()
                    self.sent.append(copy)
                    self.landing.append(post(src, target.at[origin], step, peer))
                own = source if kind == "gather" else source.at[me]
                keep(place, own, target.at[me])
            else:
                chips = size // 2
                chip, core = lax.div(me, 2), lax.rem(me, 2)
                partner = me + 1 - 2 * core
                if kind == "pair":
                    copy = post(source, target, 0, partner)
                    copy.start()
                    self.sent.append(copy)
                    self.landing.append(copy)
                    continue
                for step in range(1, chips):
                    far, origin = lax.rem(chip + step, chips), lax.rem(chip + chips - step, chips)
                    peer = 2 * far + core
                    if kind == "spread":
                        rows = source.shape[0]
                        pieces = 2 if rows % 32 == 0 else 1
                        for piece in range(pieces):
                            cut = pl.ds(piece * (rows // pieces), rows // pieces)
                            slot, later = step * pieces + piece, (size + step) * pieces + piece
                            block = target.at[2 * origin + core, cut]
                            other = target.at[2 * origin + 1 - core, cut]
                            copy = post(source.at[cut], target.at[me, cut], slot, peer)
                            arrive = post(source.at[cut], block, slot, peer)
                            onward = post(block, block, later, partner)
                            self.passing.append(
                                (piece, arrive, onward, post(block, other, later, partner))
                            )
                            copy.start()
                            self.sent.append(copy)
                        continue
                    else:
                        copy = post(source.at[far], target.at[chip], step, peer)
                        self.landing.append(
                            post(source.at[far], target.at[origin], step, peer)
                        )
                    copy.start()
                    self.sent.append(copy)
                if kind == "spread":
                    copy = post(source, target.at[me], 0, partner)
                    copy.start()
                    self.sent.append(copy)
                    self.landing.append(post(source, target.at[partner], 0, partner))
                    keep(place, source, target.at[me])
                else:
                    keep(place, source.at[chip], target.at[chip])

        for inward, outward in self.kept:
            inward.wait()
            outward.start()

    def finish(self):
        self.passing.sort(key=lambda entry: entry[0])
        for _, arrive, onward, _ in self.passing:
            arrive.wait_recv()
            onward.start()
        for _, _, onward, other in self.passing:
            onward.wait_send()
            other.wait_recv()
        for copy in self.landing:
            copy.wait_recv()
        for copy in self.sent:
            copy.wait_send()
        for _, outward in self.kept:
            outward.wait()


ANY = pl.BlockSpec(memory_space=pl.ANY)
WHOLE = pl.BlockSpec(memory_space=pltpu.VMEM)
SCALARS = pl.BlockSpec(memory_space=pltpu.SMEM)


def run_kernel(ident, name, moves, work=None, arrays=(), results=(), scratch=(), lead=None):
    transfers = Transfers(moves)
    carried, count = len(moves), len(arrays)

    def kernel(*refs):
        refs = list(refs)
        array_refs, in_refs = refs[:count], refs[count : count + carried]
        refs = refs[count + carried :]
        result_refs, out_refs = refs[: len(results)], refs[len(results) : len(results) + carried]
        refs = refs[len(results) + carried :]
        scratch_refs, refs = refs[: len(scratch)], refs[len(scratch) :]
        work_refs = (*array_refs, *result_refs, *scratch_refs)

        def begin():
            if lead is not None:
                lead(*work_refs)

        transfers.start(in_refs, out_refs, refs[:carried], refs[carried:], begin)
        if work is not None:
            work(*work_refs)
        transfers.finish()

    return pl.pallas_call(
        kernel,
        out_shape=tuple(results) + tuple(transfers.shapes()),
        in_specs=[SCALARS if value.ndim == 1 else WHOLE for value in arrays] + [ANY] * carried,
        out_specs=tuple([WHOLE] * len(results) + [ANY] * carried),
        scratch_shapes=list(scratch) + transfers.staging() + transfers.scratch(),
        compiler_params=pltpu.CompilerParams(
            collective_id=ident,
            has_side_effects=True,
            vmem_limit_bytes=VMEM_BYTES if work is not None else VMEM_BYTES // 4,
        ),
        name=name,
    )(*arrays, *[value for value, _, _ in moves])


def same_document(doc_starts, first, count, query_index):
    def segment_of(index):
        begun = jnp.zeros(index.shape, jnp.int32)
        for doc in range(doc_starts.shape[0]):
            begun += (index >= doc_starts[doc]).astype(jnp.int32)
        return begun

    key_index = first + lax.broadcasted_iota(jnp.int32, (count, 1), 0)
    return segment_of(key_index) == segment_of(query_index)


def attend_forward(
    doc_starts, keys_values, turned_pairs, turned_query, query_index, out, log_total, held
):
    total = keys_values.shape[0]
    wide = turned_query.shape[1]
    held[...] = jnp.zeros_like(held)
    query = turned_query[...]
    mine = query_index[...]

    def step(index, carry):
        highest, summed = carry
        rows = pl.ds(pl.multiple_of(index * FWD_CHUNK, FWD_CHUNK), FWD_CHUNK)
        scores = jnp.dot(keys_values[rows, :], query, preferred_element_type=jnp.float32)
        shared = same_document(doc_starts, index * FWD_CHUNK, FWD_CHUNK, mine)
        scores = jnp.where(shared, scores, MASKED)
        raised = jnp.maximum(highest, jnp.max(scores, axis=0, keepdims=True))
        lowered = jnp.exp(highest - raised)
        weights = jnp.exp(scores - raised)
        summed = summed * lowered + jnp.sum(weights, axis=0, keepdims=True)
        held[...] = held[...] * lowered + jnp.dot(
            turned_pairs[HEAD_DIM:, rows],
            weights.astype(jnp.bfloat16),
            preferred_element_type=jnp.float32,
        )
        return (raised, summed)

    highest, summed = lax.fori_loop(
        0,
        total // FWD_CHUNK,
        step,
        (jnp.full((1, wide), MASKED, jnp.float32), jnp.zeros((1, wide), jnp.float32)),
    )
    out[...] = held[...] / summed
    log_total[...] = highest + jnp.log(summed)


def attend_backward(
    doc_starts,
    keys_values,
    turned_pairs,
    turned_query,
    turned_grad,
    query_wide,
    grad_wide,
    query_index,
    log_total,
    attended,
    pair_grad,
    query_grad,
):
    total = keys_values.shape[0]
    query_grad[...] = jnp.zeros_like(query_grad)
    query = turned_query[...]
    grad = turned_grad[...]
    mine = query_index[...]
    logs = log_total[...]
    delta = jnp.sum(grad[HEAD_DIM:, :].astype(jnp.float32) * attended[...], axis=0, keepdims=True)

    def step(index, carry):
        rows = pl.ds(pl.multiple_of(index * BWD_CHUNK, BWD_CHUNK), BWD_CHUNK)
        pairs = keys_values[rows, :]
        scores = jnp.dot(pairs, query, preferred_element_type=jnp.float32)
        shared = same_document(doc_starts, index * BWD_CHUNK, BWD_CHUNK, mine)
        weights = jnp.exp(jnp.where(shared, scores - logs, MASKED))
        weight_grad = jnp.dot(pairs, grad, preferred_element_type=jnp.float32)
        score_grad = (weights * (weight_grad - delta)).astype(jnp.bfloat16)
        pair_grad[rows, :] = (
            jnp.dot(score_grad, query_wide[...], preferred_element_type=jnp.float32)
            + jnp.dot(
                weights.astype(jnp.bfloat16), grad_wide[...], preferred_element_type=jnp.float32
            )
        ).astype(pair_grad.dtype)
        query_grad[...] += jnp.dot(
            turned_pairs[:HEAD_DIM, rows], score_grad, preferred_element_type=jnp.float32
        )
        return carry

    lax.fori_loop(0, total // BWD_CHUNK, step, 0)


def one_axis(axis, held, sems):
    size = lax.axis_size(axis)
    me = lax.axis_index(axis)

    def copy(step, place):
        return pltpu.make_async_remote_copy(
            src_ref=held.at[me],
            dst_ref=held.at[place],
            send_sem=sems.at[0, step],
            recv_sem=sems.at[1, step],
            device_id={axis: lax.rem(me + step, size)},
            device_id_type=MESH,
        )

    sent = [copy(step, me) for step in range(1, size)]
    coming = [copy(step, lax.rem(me + size - step, size)) for step in range(1, size)]
    return sent, coming


def sum_lead(terms, total, over_tensor, over_shard, tensor_sems, shard_sems):
    over_tensor[lax.axis_index("tensor")] = terms[...]
    sent, coming = one_axis("tensor", over_tensor, tensor_sems)
    for copy in sent:
        copy.start()
    for copy in coming:
        copy.wait_recv()
    for copy in sent:
        copy.wait_send()
    over_shard[lax.axis_index("shard")] = jnp.sum(over_tensor[...], axis=0)
    sent, _ = one_axis("shard", over_shard, shard_sems)
    for copy in sent:
        copy.start()


def sum_everywhere(terms, total, over_tensor, over_shard, tensor_sems, shard_sems):
    sent, coming = one_axis("shard", over_shard, shard_sems)
    for copy in coming:
        copy.wait_recv()
    for copy in sent:
        copy.wait_send()
    total[...] = jnp.sum(over_shard[...], axis=0)


def fold_rows(values, padded):
    half = values.shape[-2] // 2
    folded = jnp.concatenate([values[..., :half, :], values[..., half:, :]], axis=-1)
    extra = padded - half
    if extra:
        folded = jnp.pad(folded, [(0, 0)] * (folded.ndim - 2) + [(0, extra), (0, 0)])
    return folded


def unfold_rows(folded, half):
    folded = folded[..., :half, :]
    return jnp.concatenate([folded[..., :HEAD_DIM], folded[..., HEAD_DIM:]], axis=-2)


def on_device(
    tokens,
    doc_starts,
    norm1_gain,
    qkv_weight,
    out_weight,
    norm2_gain,
    in_weight,
    down_weight,
    cotangent,
):
    row_count, model_width = tokens.shape
    local_width = qkv_weight.shape[2]
    unit_width = in_weight.shape[2]
    head_dim = HEAD_DIM
    heads = local_width // head_dim
    shards = lax.axis_size("shard")
    tensors = lax.axis_size("tensor")
    me_shard = lax.axis_index("shard")
    group_rows = row_count * tensors
    all_rows = group_rows * shards
    parts = shards // heads
    part_rows = group_rows // parts
    half = part_rows // 2
    padded = -(-half // 16) * 16
    query_rows = shards * part_rows
    group_index = me_shard * group_rows + jnp.arange(group_rows, dtype=jnp.int32)
    segment, position = doc_layout(group_index, doc_starts)
    cosine, sine = turning(position, head_dim)
    contract_rows = (((0,), (0,)), ((), ()))
    contract_cols = (((1,), (1,)), ((), ()))
    shape_heads = (group_rows, heads, head_dim)
    bf16, f32 = jnp.bfloat16, jnp.float32

    def to_parts(values):
        return (
            values.reshape(parts, part_rows, heads, head_dim)
            .transpose(2, 0, 1, 3)
            .reshape(shards, part_rows, head_dim)
        )

    def from_parts(values):
        return (
            values.reshape(heads, parts, part_rows, head_dim)
            .transpose(1, 2, 0, 3)
            .reshape(group_rows, local_width)
        )

    resid_in = tokens.astype(f32)
    normed_one, norm_one_back = jax.vjp(norm_rows, resid_in, norm1_gain)
    rows_one, qkv_full, out_full = run_kernel(
        1,
        "gather_inputs",
        [
            (normed_one.astype(bf16), "tensor", "gather"),
            (qkv_weight.reshape(-1, 3 * local_width), "shard", "spread"),
            (out_weight, "shard", "spread"),
        ],
    )
    rows_one = rows_one.reshape(group_rows, model_width)
    qkv_mat = qkv_full.reshape(model_width, 3 * local_width)
    projected = jnp.dot(rows_one, qkv_mat, preferred_element_type=f32)
    score_scale = head_dim ** (-0.5)
    query = rotate(projected[:, :local_width].reshape(shape_heads), cosine, sine, 1.0).astype(bf16)
    keys = rotate(
        projected[:, local_width : 2 * local_width].reshape(shape_heads), cosine, sine, 1.0
    ).astype(bf16)
    values = projected[:, 2 * local_width :].astype(bf16).reshape(shape_heads)
    pairs = jnp.concatenate([keys, values], axis=-1).transpose(1, 0, 2)
    pairs = jnp.broadcast_to(pairs[:, None], (heads, parts, group_rows, 2 * head_dim)).reshape(
        shards, group_rows, 2 * head_dim
    )
    folded_query = fold_rows(to_parts(query * jnp.asarray(score_scale, bf16)), padded)
    early = row_count // 32 * 16
    sent_qkv, cot_early = run_kernel(
        2,
        "swap_heads",
        [
            (jnp.concatenate([pairs, folded_query], axis=1), "shard", "swap"),
            (cotangent[:early], "tensor", "gather"),
        ],
    )
    out_full = out_full.reshape(model_width, local_width)
    keys_values = sent_qkv[:, :group_rows].reshape(all_rows, 2 * head_dim)
    turned_pairs = keys_values.T
    query_mine = unfold_rows(sent_qkv[:, group_rows:], half).reshape(query_rows, head_dim)
    no_query = jnp.zeros_like(query_mine)
    query_wide = jnp.concatenate([query_mine, no_query], axis=1)
    turned_query = query_wide.T
    query_index = (
        jnp.arange(shards, dtype=jnp.int32)[:, None] * group_rows
        + lax.rem(me_shard, parts) * part_rows
        + jnp.arange(part_rows, dtype=jnp.int32)[None, :]
    ).reshape(1, query_rows)
    attended_turned, log_total, down_full, cot_late = run_kernel(
        3,
        "attend_forward",
        [
            (down_weight, "shard", "spread"),
            (cotangent[early:], "tensor", "gather"),
        ],
        attend_forward,
        (doc_starts, keys_values, turned_pairs, turned_query, query_index),
        (
            jax.ShapeDtypeStruct((head_dim, query_rows), f32),
            jax.ShapeDtypeStruct((1, query_rows), f32),
        ),
        (pltpu.VMEM((head_dim, query_rows), f32),),
    )
    cot_full = jnp.concatenate([cot_early, cot_late], axis=1).reshape(group_rows, model_width)
    attended_back = fold_rows(
        attended_turned.astype(bf16).T.reshape(shards, part_rows, head_dim), padded
    )
    (attended_parts,) = run_kernel(4, "return_heads", [(attended_back, "shard", "swap")])
    attended = from_parts(unfold_rows(attended_parts, half))

    def share(left, right):
        return (
            lax.dot_general(left, right, contract_cols, preferred_element_type=f32)
            .astype(bf16)
            .reshape(tensors, row_count, model_width)
        )

    out_parts, in_full = run_kernel(
        5,
        "out_shares",
        [
            (share(attended, out_full), "tensor", "swap"),
            (in_weight.reshape(-1, 2 * unit_width), "shard", "spread"),
        ],
    )
    down_full = down_full.reshape(model_width, unit_width)
    in_mat = in_full.reshape(model_width, 2 * unit_width)
    resid_mid = resid_in + jnp.sum(out_parts.astype(f32), axis=0)
    normed_two, norm_two_back = jax.vjp(norm_rows, resid_mid, norm2_gain)
    (rows_two,) = run_kernel(6, "gather_middle", [(normed_two.astype(bf16), "tensor", "gather")])
    rows_two = rows_two.reshape(group_rows, model_width)
    gate_up = jnp.dot(rows_two, in_mat, preferred_element_type=f32)
    active, geglu_back = jax.vjp(geglu, gate_up[:, :unit_width], gate_up[:, unit_width:])
    active = active.astype(bf16)
    active_grad = jnp.dot(cot_full, down_full, preferred_element_type=f32)
    gate_grad, up_grad = geglu_back(active_grad)
    gate_up_grad = jnp.concatenate([gate_grad, up_grad], axis=1).astype(bf16)
    core = lax.rem(me_shard, 2)
    block_rows = model_width // shards

    def core_columns(values):
        split = values.reshape(group_rows, shards // 2, 2, block_rows)
        even = split[:, :, 0].reshape(group_rows, -1)
        odd = split[:, :, 1].reshape(group_rows, -1)
        return jnp.where(core == 0, even, odd), jnp.where(core == 0, odd, even)

    def weight_grad(rows, grads):
        return lax.dot_general(rows, grads, contract_rows, preferred_element_type=f32)

    two_own, two_other = core_columns(rows_two)
    cot_own, cot_other = core_columns(cot_full)
    in_other = weight_grad(two_other, gate_up_grad).astype(bf16)
    down_other = weight_grad(cot_other, active).astype(bf16)
    two_parts, in_pair, down_pair = run_kernel(
        7,
        "middle_grad_shares",
        [
            (share(gate_up_grad, in_mat), "tensor", "swap"),
            (in_other, "shard", "pair"),
            (down_other, "shard", "pair"),
        ],
    )
    normed_two_grad = jnp.sum(two_parts.astype(f32), axis=0)
    mid_part, gain_two_grad = norm_two_back(normed_two_grad)
    mid_grad = cotangent.astype(f32) + mid_part
    in_sum = (weight_grad(two_own, gate_up_grad) + in_pair.astype(f32)).astype(bf16)
    in_sum = in_sum.reshape(shards // 2, block_rows, 2 * unit_width)
    branch_full, in_parts = run_kernel(
        8,
        "gather_branch",
        [
            (mid_grad.astype(bf16), "tensor", "gather"),
            (in_sum, "shard", "mates"),
        ],
    )
    branch_full = branch_full.reshape(group_rows, model_width)
    out_grad = lax.dot_general(branch_full, attended, contract_rows, preferred_element_type=f32)
    attended_grad = jnp.dot(branch_full, out_full, preferred_element_type=f32).astype(bf16)
    (grad_parts,) = run_kernel(
        9,
        "swap_grads",
        [(fold_rows(to_parts(attended_grad.reshape(shape_heads)), padded), "shard", "swap")],
    )
    grad_mine = unfold_rows(grad_parts, half).reshape(query_rows, head_dim)
    grad_wide = jnp.concatenate([jnp.zeros_like(grad_mine), grad_mine], axis=1)

    down_sum = (weight_grad(cot_own, active) + down_pair.astype(f32)).astype(bf16)
    down_sum = down_sum.reshape(shards // 2, block_rows, unit_width)
    by_shard = (shards, block_rows)
    pair_grad, query_grad_turned, mixed_parts, down_parts, out_grads = run_kernel(
        10,
        "attend_backward",
        [
            (share(active, down_full), "tensor", "swap"),
            (down_sum, "shard", "mates"),
            (out_grad.astype(bf16).reshape(*by_shard, local_width), "shard", "swap"),
        ],
        attend_backward,
        (
            doc_starts,
            keys_values,
            turned_pairs,
            turned_query,
            grad_wide.T,
            query_wide,
            grad_wide,
            query_index,
            log_total,
            attended_turned,
        ),
        (
            jax.ShapeDtypeStruct((all_rows, 2 * head_dim), bf16),
            jax.ShapeDtypeStruct((head_dim, query_rows), f32),
        ),
    )
    mixed = (resid_mid + jnp.sum(mixed_parts.astype(f32), axis=0)).astype(bf16)
    folded_grad = fold_rows(
        query_grad_turned.astype(bf16).T.reshape(shards, part_rows, head_dim), padded
    )
    (qkv_back,) = run_kernel(
        11,
        "return_grads",
        [
            (
                jnp.concatenate(
                    [pair_grad.reshape(shards, group_rows, 2 * head_dim), folded_grad], axis=1
                ),
                "shard",
                "swap",
            )
        ],
    )
    query_rot_grad = from_parts(unfold_rows(qkv_back[:, group_rows:], half)).reshape(shape_heads)
    pair_sum = jnp.sum(
        qkv_back[:, :group_rows].reshape(heads, parts, group_rows, 2 * head_dim).astype(f32), axis=1
    ).transpose(1, 0, 2)
    query_grad = rotate(query_rot_grad.astype(f32) * score_scale, cosine, sine, -1.0).astype(bf16)
    key_grad = rotate(pair_sum[..., :head_dim], cosine, sine, -1.0).astype(bf16)
    qkv_grad = jnp.concatenate(
        [
            query_grad.reshape(group_rows, local_width),
            key_grad.reshape(group_rows, local_width),
            pair_sum[..., head_dim:].astype(bf16).reshape(group_rows, local_width),
        ],
        axis=1,
    )
    qkv_grad_w = lax.dot_general(rows_one, qkv_grad, contract_rows, preferred_element_type=f32)
    one_share = lax.dot_general(qkv_grad, qkv_mat, contract_cols, preferred_element_type=f32)
    gain_one_share = jnp.sum(one_share * rows_one.astype(f32), axis=0) / norm1_gain
    gains = jnp.concatenate([gain_one_share, gain_two_grad]).reshape(-1, 128)
    gain_all, one_parts, qkv_parts = run_kernel(
        12,
        "input_grad_shares",
        [
            (one_share.astype(bf16).reshape(tensors, row_count, model_width), "tensor", "swap"),
            (qkv_grad_w.astype(bf16).reshape(*by_shard, 3 * local_width), "shard", "swap"),
        ],
        sum_everywhere,
        (gains,),
        (jax.ShapeDtypeStruct(gains.shape, f32),),
        (
            pltpu.VMEM((tensors,) + gains.shape, f32),
            pltpu.VMEM((shards,) + gains.shape, f32),
            pltpu.SemaphoreType.DMA((2, tensors)),
            pltpu.SemaphoreType.DMA((2, shards)),
        ),
        sum_lead,
    )
    gain_all = gain_all.reshape(2, model_width)
    normed_one_grad = jnp.sum(one_parts.astype(f32), axis=0)
    input_part, _ = norm_one_back(normed_one_grad)
    tokens_grad = (mid_grad + input_part).astype(bf16)

    def add_up(pieces, shape):
        return jnp.sum(pieces.astype(f32), axis=0).reshape(shape)

    return (
        mixed,
        tokens_grad,
        gain_all[0],
        add_up(qkv_parts, qkv_weight.shape),
        add_up(out_grads, out_weight.shape),
        gain_all[1],
        add_up(in_parts, in_weight.shape),
        add_up(down_parts, down_weight.shape),
    )


def solution(mesh):
    in_specs = (
        P(("shard", "tensor"), None),
        P(),
        P(),
        P("shard", None, "tensor"),
        P("shard", "tensor"),
        P(),
        P("shard", None, "tensor"),
        P("shard", "tensor"),
        P(("shard", "tensor"), None),
    )
    out_specs = (
        P(("shard", "tensor"), None),
        P(("shard", "tensor"), None),
        P(),
        P("shard", None, "tensor"),
        P("shard", "tensor"),
        P(),
        P("shard", None, "tensor"),
        P("shard", "tensor"),
    )
    return jax.shard_map(
        on_device, mesh=mesh, in_specs=in_specs, out_specs=out_specs, check_vma=False
    )
```
